512 devices in a mesh: build: 16 (over z), gx: 4 (over y), gy: 8 (over x, core).
Axes of the slice: x: 4, y: 4, z: 16, core: 2. Of those that a mesh axis runs over, the one named last changes fastest.
Arguments:
- design: float32 [64, 256, 2048], P('build', 'gx', 'gy'), may hold values from 0 to 1
- cotangent: float32 [64, 256, 2048], P('build', 'gx', 'gy'), may hold values from -6 to 6
Outputs:
- printed: float32 [64, 256, 2048], P('build', 'gx', 'gy')
- gradient: float32 [64, 256, 2048], P('build', 'gx', 'gy')
The draws below stay inside these ranges and needn't reach their ends.
All inputs are finite; a program needn't handle non-finite values.
Results may differ from the reference program's by a relative error of at most 0.00016.
Values sent between devices are 32-bit elements; how exact they have to be, the bound alone decides.
A program may use at most 64 MiB of HBM per device.

```python
import jax
import jax.numpy as jnp
from jax import lax

LAYERS = 64
NX = 256
NY = 2048


def level_of(key, shape, cuts, low, high):
    factor_of, own = 1.0, jax.random.fold_in(key, 6)
    for position, blocks in cuts:
        steps = jnp.exp(jax.random.uniform(jax.random.fold_in(own, position), (blocks,), jnp.float32, low / len(cuts), high / len(cuts)))
        factor_of = factor_of * jnp.repeat(steps, shape[position] // blocks).reshape([-1 if axis == position else 1 for axis in range(len(shape))])
    return factor_of


def bell_draw(own_key, dims, deviation, reach, shards=(), kind=jnp.bfloat16):
    result = deviation * jax.random.normal(own_key, dims, jnp.float32)
    if shards:
        result = result * level_of(own_key, dims, shards, -0.22, 0.18)
    return jnp.clip(result, -reach, reach).astype(kind)


def setup_inputs(seed: int = 0) -> dict:
    key_of = jax.random.split(jax.random.key(seed), 3)
    design = jnp.clip(1.0 * jax.random.uniform(key_of[0], (LAYERS, NX, NY), jnp.float32) ** level_of(key_of[0], (LAYERS, NX, NY), ((0, 16), (1, 4), (2, 8)), -0.2, 0.2), 0.0, 1.0)
    cotangent = bell_draw(key_of[1], (LAYERS, NX, NY), 1.0, 6.0, ((0, 16), (1, 4), (2, 8)), jnp.float32)
    return {"design": design, "cotangent": cotangent}


SHARPNESS = 40.0
SOFTNESS = 0.0001
SOFT_ROOT = 0.01

def shifted_sum(padded):
    return padded[1:-1, 1:-1] + padded[:-2, 1:-1] + padded[2:, 1:-1] + padded[1:-1, :-2] + padded[1:-1, 2:]

def soft_terms(stratum, lower):
    totals = shifted_sum(jnp.exp(SHARPNESS * jnp.pad(lower, 1)))
    bounds = jnp.log(totals / 5.0) / SHARPNESS
    excess = stratum - bounds
    radius = jnp.sqrt(excess * excess + SOFTNESS)
    return (totals, bounds, excess, radius)

def reference(design, cotangent):
    base_plate = jnp.ones_like(design[0])

    def forward(lower, stratum):
        totals, bounds, excess, radius = soft_terms(stratum, lower)
        fresh = 0.5 * (stratum + bounds - radius + SOFT_ROOT)
        return (fresh, fresh)
    _, printed = lax.scan(forward, base_plate, design)
    lowers = jnp.concatenate([base_plate[None], printed[:-1]], 0)

    def backward(pullback, inputs):
        stratum, lower, current, weight = inputs
        totals, bounds, excess, radius = soft_terms(stratum, lower)
        adjoint = weight + jnp.exp(SHARPNESS * current) * shifted_sum(jnp.pad(pullback, 1))
        gradient = adjoint * 0.5 * (1.0 - excess / radius)
        pullback = adjoint * 0.5 * (1.0 + excess / radius) / totals
        return (pullback, gradient)
    _, gradient = lax.scan(backward, jnp.zeros_like(design[0]), (design, lowers, printed, cotangent), reverse=True)
    return (printed, gradient)
```

```python
import math

import jax
import jax.numpy as jnp
from jax import lax
from jax.experimental import pallas as pl
from jax.experimental.pallas import tpu as pltpu
from jax.sharding import PartitionSpec as P

MESH = pl.DeviceIdType.MESH
SHARPNESS = 40.0
SOFTNESS = 0.0001
SOFT_ROOT = 0.01
LOG2_E = 1.0 / math.log(2.0)

GROUP = 4
OWN = 4
DEPTH = GROUP * OWN
ROWS = 64
COLS = 256
BAND = ROWS // GROUP
REGION = 3 * BAND
WIDE = COLS + 128
KEPT = 7
LATE = DEPTH - KEPT


def five(v):
    rows = v.shape[0]
    return (
        v
        + pltpu.roll(v, 1, axis=0)
        + pltpu.roll(v, rows - 1, axis=0)
        + pltpu.roll(v, 1, axis=1)
        + pltpu.roll(v, WIDE - 1, axis=1)
    )


def kernel(
    d_ref, c_ref, pr_ref, gr_ref,
    edge, edge_in, wrap, big, bigwrap, weights, ends, ends_in, late_ends, late_in,
    top, top_in, pst, gst, a1, a2, inside_ref,
    swap_s, swap_r, wrap_s, wrap_r, edge_s, edge_r, hand_s, hand_r, back_s, back_r,
    late_s, late_r, out_s, out_r,
):
    zb, y, g = lax.axis_index("build"), lax.axis_index("gx"), lax.axis_index("gy")
    stages, gys = lax.axis_size("build") // GROUP, lax.axis_size("gy")
    blocks = lax.axis_size("gx") * GROUP
    s, place = zb // GROUP, zb % GROUP

    def flip(row, v):
        return v + (row % 2) * (GROUP - 1 - 2 * v)

    r = flip(y, place)
    block = GROUP * y + r

    def owner(stage, blk, gy):
        row = blk // GROUP
        return {"build": GROUP * stage + flip(row, blk % GROUP), "gx": row, "gy": gy}

    def start(src, dst, send, recv, dev):
        pltpu.make_async_remote_copy(
            src_ref=src, dst_ref=dst, send_sem=send, recv_sem=recv, device_id=dev, device_id_type=MESH
        ).start()

    def wait(ref, sem):
        pltpu.make_async_copy(ref, ref, sem).wait()

    def flag(c):
        return jnp.where(c, 1, 0)

    barrier = pltpu.get_barrier_semaphore()
    count = jnp.int32(0)

    def greet(dev, valid):
        @pl.when(valid)
        def _():
            pl.semaphore_signal(barrier, inc=1, device_id=dev, device_id_type=MESH)

        return flag(valid)

    def near(blk, gy):
        return (blk >= 0) & (blk < blocks) & (gy >= 0) & (gy < gys)

    for dy in (-1, 0, 1):
        for p in range(GROUP):
            valid = (y + dy >= 0) & (y + dy < blocks // GROUP)
            if dy == 0:
                valid = valid & (p != place)
            count += greet({"build": GROUP * s + p, "gx": y + dy, "gy": g}, valid)
    for dg in (-1, 1):
        for db in (-1, 0, 1):
            count += greet(owner(s, block + db, g + dg), near(block + db, g + dg))
    for ds in (-1, 1):
        for dg in (-1, 0, 1):
            for db in (-1, 0, 1):
                valid = near(block + db, g + dg) & (s + ds >= 0) & (s + ds < stages)
                count += greet(owner(s + ds, block + db, g + dg), valid)

    lane = lax.broadcasted_iota(jnp.int32, (ROWS, 128), 1)
    for which, ref in enumerate((d_ref, c_ref)):
        packed = jnp.zeros((ROWS, 128), jnp.float32)
        for i in range(OWN):
            both = jnp.where(lane < 64, ref[i, :, 0:128], ref[i, :, 128:256])
            if i:
                both = pltpu.roll(both, 32 * i, axis=1)
            slot = (lane + 16 - 32 * i + 128) % 128
            packed = jnp.where(slot < 32, both, packed)
        edge[which] = packed
    row = lax.broadcasted_iota(jnp.int32, (REGION, WIDE), 0) + (block - 1) * BAND
    col = lax.broadcasted_iota(jnp.int32, (REGION, WIDE), 1)
    col = jnp.where(col < COLS + 64, col, col - WIDE) + g * COLS
    within = (row >= 0) & (row < blocks * BAND) & (col >= 0) & (col < gys * COLS)
    inside_ref[...] = jnp.where(within, 1.0, 0.0)

    pl.semaphore_wait(barrier, count)

    def edge_send(which, go):
        for side, dg in ((0, 1), (1, -1)):

            @pl.when((g + dg >= 0) & (g + dg < gys))
            def _():
                if go:
                    start(edge.at[which], edge_in.at[which, side], edge_s.at[which, side], edge_r.at[which, side],
                          {"build": zb, "gx": y, "gy": g + dg})
                else:
                    wait(edge.at[which], edge_s.at[which, side])

    def edge_land(which):
        for side, dg in ((0, -1), (1, 1)):

            @pl.when((g + dg >= 0) & (g + dg < gys))
            def _():
                wait(edge_in.at[which, side], edge_r.at[which, side])

        wrap[which] = jnp.where(lane % 32 < 16, edge_in[which, 1], edge_in[which, 0])

    def swap(which, narrow, go):
        def step(rp, _):
            rows = pl.ds(pl.multiple_of(rp * BAND, BAND), BAND)
            for db in (-1, 0, 1):
                target = GROUP * y + rp + db
                there = pl.ds((1 - db) * BAND, BAND)
                if narrow:
                    src = wrap.at[which, rows]
                    dst = bigwrap.at[which, place, there]
                    send, recv = wrap_s.at[which, rp, db + 1], wrap_r.at[which, place, 1 - db]
                else:
                    src = (d_ref, c_ref)[which].at[:, rows]
                    dst = big.at[which, pl.ds(OWN * place, OWN), there]
                    send, recv = swap_s.at[which, rp, db + 1], swap_r.at[which, place, 1 - db]

                @pl.when((target >= 0) & (target < blocks) & (target != block))
                def _():
                    if go:
                        start(src, dst, send, recv, owner(s, target, g))
                    else:
                        wait(src, send)

                if go:

                    @pl.when(target == block)
                    def _():
                        pltpu.make_async_copy(src, dst, recv).start()

            return 0

        lax.fori_loop(0, GROUP, step, 0)

    def swap_land(which, p):
        for b in range(3):
            there = pl.ds(b * BAND, BAND)

            @pl.when((block + b - 1 >= 0) & (block + b - 1 < blocks))
            def _():
                wait(big.at[which, pl.ds(OWN * p, OWN), there], swap_r.at[which, p, b])
                wait(bigwrap.at[which, p, there], wrap_r.at[which, p, b])

    edge_send(0, True)
    swap(0, False, True)
    edge_send(1, True)
    edge_land(0)
    swap(0, True, True)
    swap(1, False, True)
    edge_land(1)
    swap(1, True, True)

    def hand(up, go):
        which = 0 if up else 1
        ds = 1 if up else -1
        send = hand_s if up else back_s
        recv = hand_r if up else back_r
        for db in (-1, 0, 1):
            for dg in (0, -1, 1):
                there = pl.ds((1 - db) * BAND, BAND)
                if dg == 0:
                    src, dst = top.at[which], top_in.at[which, there]
                else:
                    src, dst = ends.at[which], ends_in.at[which, 0 if dg == 1 else 1, there]

                @pl.when(near(block + db, g + dg) & (s + ds >= 0) & (s + ds < stages))
                def _():
                    if go:
                        start(src, dst, send.at[1 - db, 1 - dg], recv.at[1 - db, 1 - dg],
                              owner(s + ds, block + db, g + dg))
                    else:
                        wait(src, send.at[1 - db, 1 - dg])

    def hand_land(up):
        which = 0 if up else 1
        ds = -1 if up else 1
        recv = hand_r if up else back_r
        for b in range(3):
            for e in range(3):
                there = pl.ds(b * BAND, BAND)
                if e == 1:
                    dst = top_in.at[which, there]
                else:
                    dst = ends_in.at[which, 0 if e == 0 else 1, there]

                @pl.when(near(block + b - 1, g + e - 1) & (s + ds >= 0) & (s + ds < stages))
                def _():
                    wait(dst, recv.at[b, e])

    lane_region = lax.broadcasted_iota(jnp.int32, (REGION, 128), 1)
    lane_band = lax.broadcasted_iota(jnp.int32, (BAND, 128), 1)

    def handed(which):
        tail = jnp.where(lane_region < 64, ends_in[which, 1], ends_in[which, 0])
        return jnp.concatenate([top_in[which], tail], axis=1)

    def give(which, value):
        top[which] = value
        ends[which] = jnp.where(lane_band < 64, value[:, 0:128], value[:, 128:256])

    def field(which, p, i, lo, hi):
        tail = bigwrap[which, p, lo:hi]
        if i:
            tail = pltpu.roll(tail, 128 - 32 * i, axis=1)
        return jnp.concatenate([big[which, OWN * p + i, lo:hi], tail], axis=1)

    def terms(total, des):
        bound = jnp.log2(total) * (1.0 / (LOG2_E * SHARPNESS)) - math.log(5.0) / SHARPNESS
        excess = des - bound
        under = excess * excess + SOFTNESS
        return bound, excess, under, lax.rsqrt(under)

    hand_land(True)
    inside = inside_ref[...] > 0.5
    first = jnp.where(s > 0, handed(0), jnp.full((REGION, WIDE), math.exp(SHARPNESS), jnp.float32))
    first = jnp.where(inside, first, 1.0)
    weights[0] = first

    def forward(lo, hi, p, w):
        swap_land(0, p)
        mask = inside_ref[lo:hi] > 0.5
        for i in range(OWN):
            des = field(0, p, i, lo, hi)
            bound, excess, under, inverse = terms(five(w), des)
            fresh = 0.5 * (des + bound - under * inverse + SOFT_ROOT)
            w = jnp.where(mask, jnp.exp2(fresh * (SHARPNESS * LOG2_E)), 1.0)
            pst[OWN * p + i] = fresh[BAND - lo : 2 * BAND - lo, 0:COLS]
            j = OWN * p + i
            if lo == 0 and i < OWN - 1:
                weights[j + 1] = w
            elif lo == 0:

                @pl.when(p == 0)
                def _():
                    weights[j + 1] = w

                @pl.when(p > 0)
                def _():
                    weights[j + 1, BAND : 2 * BAND, 0:COLS] = w[BAND : 2 * BAND, 0:COLS]

            else:
                weights[j + 1, BAND : 2 * BAND, 0:COLS] = w[BAND - lo : 2 * BAND - lo, 0:COLS]
        return w

    half = BAND // 2
    w = lax.fori_loop(0, 2, lambda p, w: forward(0, REGION, p, w), first)
    w = w[half : REGION - half]
    w = lax.fori_loop(2, 4, lambda p, w: forward(half, REGION - half, p, w), w)
    give(0, w[half : half + BAND, 0:COLS])
    hand(True, True)

    own = weights[KEPT + 1 :, BAND : 2 * BAND, 0:COLS]
    lane_late = lax.broadcasted_iota(jnp.int32, (LATE, BAND, 128), 2)
    late_ends[...] = jnp.where(lane_late < 64, own[:, :, 0:128], own[:, :, 128:256])

    def late(go):
        for db in (-1, 0, 1):
            for dg in (0, -1, 1):
                if db == 0 and dg == 0:
                    continue
                there = pl.ds((1 - db) * BAND, BAND)
                if dg == 0:
                    src = weights.at[pl.ds(KEPT + 1, LATE), pl.ds(BAND, BAND), pl.ds(0, COLS)]
                    dst = weights.at[pl.ds(KEPT + 1, LATE), there, pl.ds(0, COLS)]
                else:
                    src, dst = late_ends, late_in.at[0 if dg == 1 else 1, :, there]

                @pl.when(near(block + db, g + dg))
                def _():
                    if go:
                        start(src, dst, late_s.at[1 - db, 1 - dg], late_r.at[1 - db, 1 - dg],
                              owner(s, block + db, g + dg))
                    else:
                        wait(src, late_s.at[1 - db, 1 - dg])

    def late_land():
        for b in range(3):
            for e in range(3):
                if b == 1 and e == 1:
                    continue
                there = pl.ds(b * BAND, BAND)
                if e == 1:
                    dst = weights.at[pl.ds(KEPT + 1, LATE), there, pl.ds(0, COLS)]
                else:
                    dst = late_in.at[0 if e == 0 else 1, :, there]

                @pl.when(near(block + b - 1, g + e - 1))
                def _():
                    wait(dst, late_r.at[b, e])

    late(True)

    def result(which, p, go):
        src_ref, dst_ref = (pst, gst)[which], (pr_ref, gr_ref)[which]
        src = src_ref.at[pl.ds(OWN * p, OWN)]
        dst = dst_ref.at[:, pl.ds(pl.multiple_of(r * BAND, BAND), BAND)]

        @pl.when(p != place)
        def _():
            if go:
                start(src, dst, out_s.at[which, p], out_r.at[which, r], {"build": GROUP * s + p, "gx": y, "gy": g})
            else:
                wait(src, out_s.at[which, p])

        if go:

            @pl.when(p == place)
            def _():
                pltpu.make_async_copy(src, dst, out_r.at[which, r]).start()

    for p in range(GROUP):
        result(0, p, True)

    late_land()

    def fill(n, _):
        j = n + KEPT + 1
        tail = jnp.where(lane_region < 64, late_in[1, n], late_in[0, n])
        weights[j, :, COLS:] = jnp.where(inside_ref[:, COLS:] > 0.5, tail, 1.0)
        for rows in (slice(0, BAND), slice(2 * BAND, REGION)):
            weights[j, rows, 0:COLS] = jnp.where(inside_ref[rows, 0:COLS] > 0.5, weights[j, rows, 0:COLS], 1.0)
        return 0

    lax.fori_loop(0, LATE, fill, 0)

    def prepare(lo, hi, p, _):
        for i in range(OWN):
            j = OWN * p + i
            total = five(weights[j, lo:hi])
            bound, excess, under, inverse = terms(total, field(0, p, i, lo, hi))
            ratio = excess * inverse
            a1[j, lo:hi] = jnp.where(inside_ref[lo:hi] > 0.5, 0.5 * (1.0 + ratio) / total, 0.0)
            a2[j] = 0.5 * (1.0 - ratio[BAND - lo : 2 * BAND - lo, 0:COLS])
        return 0

    lax.fori_loop(0, 2, lambda p, _: prepare(half, REGION - half, p, _), 0)
    lax.fori_loop(2, 4, lambda p, _: prepare(0, REGION, p, _), 0)

    for p in range(GROUP):
        swap_land(1, p)
    hand_land(False)
    q = jnp.where((s < stages - 1) & inside, handed(1), 0.0)

    def backward(lo, hi, n, q):
        p = GROUP - 1 - n
        mask = inside_ref[lo:hi] > 0.5
        for i in range(OWN - 1, -1, -1):
            j = OWN * p + i
            adjoint = field(1, p, i, lo, hi) + weights[j + 1, lo:hi] * five(q)
            gst[j] = adjoint[BAND - lo : 2 * BAND - lo, 0:COLS] * a2[j]
            q = jnp.where(mask, adjoint * a1[j, lo:hi], 0.0)
        return q

    q = lax.fori_loop(0, 2, lambda n, q: backward(0, REGION, n, q), q)
    q = q[half : REGION - half]
    q = lax.fori_loop(2, 4, lambda n, q: backward(half, REGION - half, n, q), q)
    give(1, q[half : half + BAND, 0:COLS])
    hand(False, True)
    for p in range(GROUP):
        result(1, p, True)

    for which in range(2):
        edge_send(which, False)
        swap(which, False, False)
        swap(which, True, False)
        for p in range(GROUP):
            result(which, p, False)
    hand(True, False)
    hand(False, False)
    late(False)
    for which in range(2):
        for p in range(GROUP):
            rows = pl.ds(BAND * p, BAND)
            wait((pr_ref, gr_ref)[which].at[:, rows], out_r.at[which, p])


def local(design, cotangent):
    shard = jax.ShapeDtypeStruct(design.shape, jnp.float32)
    f32 = lambda *shape: pltpu.VMEM(shape, jnp.float32)
    dma = lambda *shape: pltpu.SemaphoreType.DMA(shape)
    vmem = pl.BlockSpec(memory_space=pltpu.VMEM)
    return pl.pallas_call(
        kernel,
        out_shape=(shard, shard),
        in_specs=[vmem, vmem],
        out_specs=(vmem, vmem),
        scratch_shapes=[
            f32(2, ROWS, 128),
            f32(2, 2, ROWS, 128),
            f32(2, ROWS, 128),
            f32(2, DEPTH, REGION, COLS),
            f32(2, GROUP, REGION, 128),
            f32(DEPTH + 1, REGION, WIDE),
            f32(2, BAND, 128),
            f32(2, 2, REGION, 128),
            f32(LATE, BAND, 128),
            f32(2, LATE, REGION, 128),
            f32(2, BAND, COLS),
            f32(2, REGION, COLS),
            f32(DEPTH, BAND, COLS),
            f32(DEPTH, BAND, COLS),
            f32(DEPTH, REGION, WIDE),
            f32(DEPTH, BAND, COLS),
            f32(REGION, WIDE),
            dma(2, GROUP, 3),
            dma(2, GROUP, 3),
            dma(2, GROUP, 3),
            dma(2, GROUP, 3),
            dma(2, 2),
            dma(2, 2),
            dma(3, 3),
            dma(3, 3),
            dma(3, 3),
            dma(3, 3),
            dma(3, 3),
            dma(3, 3),
            dma(2, GROUP),
            dma(2, GROUP),
        ],
        compiler_params=pltpu.CompilerParams(
            collective_id=0, has_side_effects=True, vmem_limit_bytes=40 * 1024 * 1024
        ),
    )(design, cotangent)


def solution(mesh):
    spec = P("build", "gx", "gy")
    return jax.shard_map(local, mesh=mesh, in_specs=(spec, spec), out_specs=(spec, spec), check_vma=False)
```

```python
import math

import jax
import jax.numpy as jnp
from jax import lax
from jax.experimental import pallas as pl
from jax.experimental.pallas import tpu as pltpu
from jax.sharding import PartitionSpec as P

MESH = pl.DeviceIdType.MESH
SHARPNESS = 40.0
SOFTNESS = 0.0001
SOFT_ROOT = 0.01
LOG2_E = 1.0 / math.log(2.0)

OWN = 4
ROWS = 64
STRIP = 16
REGION = 3 * STRIP
LANES = 128
DEPTH = 16
PAIRS = DEPTH // 2
DESIGN, COTANGENT, WEIGHT = range(3)


def five(v):
    cols = v.shape[0]
    return (
        v
        + pltpu.roll(v, 1, axis=0)
        + pltpu.roll(v, cols - 1, axis=0)
        + pltpu.roll(v, 1, axis=1)
        + pltpu.roll(v, LANES - 1, axis=1)
    )


def turned(v, shift):
    return pltpu.roll(v, shift % LANES, axis=1) if shift % LANES else v


def kernel(
    d_ref, c_ref, pr_ref, gr_ref,
    raw, nat, ext, band_out, band_in, weights, a1, a2, results, home, sync_out, sync_in, inside_ref,
    raw_sem, swap_s, swap_r, col_s, col_r, band_s, band_r, sync_s, sync_r, out_s, out_r,
):
    z, y, g = lax.axis_index("build"), lax.axis_index("gx"), lax.axis_index("gy")
    planes, xs, gys = lax.axis_size("build"), lax.axis_size("gx"), lax.axis_size("gy")
    strips = planes * gys
    segments = planes * OWN // DEPTH
    per_segment = DEPTH // OWN

    def flip(column, v):
        return v + (column % 2) * (planes - 1 - 2 * v)

    k = flip(g, z)
    strip = planes * g + k

    def owner(number, row):
        column = number // planes
        return {"build": flip(column, number % planes), "gx": row, "gy": column}

    def near(ds, dy):
        return (strip + ds >= 0) & (strip + ds < strips) & (y + dy >= 0) & (y + dy < xs)

    def start(src, dst, send, recv, dev):
        pltpu.make_async_remote_copy(
            src_ref=src, dst_ref=dst, send_sem=send, recv_sem=recv, device_id=dev, device_id_type=MESH
        ).start()

    def wait(ref, sem):
        pltpu.make_async_copy(ref, ref, sem).wait()

    for which, ref in ((DESIGN, d_ref), (COTANGENT, c_ref)):
        pltpu.make_async_copy(ref, raw.at[which], raw_sem.at[which]).start()

    barrier = pltpu.get_barrier_semaphore()
    count = jnp.int32(planes - 1)

    def greet(p, _):
        @pl.when(p != z)
        def _():
            pl.semaphore_signal(barrier, inc=1, device_id={"build": p, "gx": y, "gy": g}, device_id_type=MESH)

        return 0

    lax.fori_loop(0, planes, greet, 0)
    for ds in (-1, 0, 1):
        for dy in (-1, 0, 1):
            if ds == 0 and dy == 0:
                continue
            valid = near(ds, dy)
            if dy == 0:
                valid = valid & ((strip + ds) // planes != g)

            @pl.when(valid)
            def _():
                pl.semaphore_signal(barrier, inc=1, device_id=owner(strip + ds, y + dy), device_id_type=MESH)

            count += jnp.where(valid, 1, 0)

    lane = lax.broadcasted_iota(jnp.int32, (REGION, LANES), 1)
    row = jnp.where(lane < 96, lane, lane - LANES) + y * ROWS
    col = lax.broadcasted_iota(jnp.int32, (REGION, LANES), 0) + (strip - 1) * STRIP
    within = (row >= 0) & (row < xs * ROWS) & (col >= 0) & (col < strips * STRIP)
    inside_ref[...] = jnp.where(within, 1.0, 0.0)

    def transpose_in(which):
        wait(raw.at[which], raw_sem.at[which])
        for n in range(OWN // 2):
            both = jnp.concatenate([raw[which, 2 * n], raw[which, 2 * n + 1]], axis=0)
            nat[which, n] = both.T

    transpose_in(DESIGN)
    pl.semaphore_wait(barrier, count)

    def swap(which, go):
        def step(i, _):
            p = (z + i) % planes
            src = nat.at[which, :, pl.ds(pl.multiple_of(flip(g, p) * STRIP, STRIP), STRIP)]
            dst = ext.at[which, pl.ds(2 * z, 2), pl.ds(STRIP, STRIP)]

            @pl.when(p != z)
            def _():
                if go:
                    start(src, dst, swap_s.at[which, p], swap_r.at[which, z], {"build": p, "gx": y, "gy": g})
                else:
                    wait(src, swap_s.at[which, p])

            if go:

                @pl.when(p == z)
                def _():
                    pltpu.make_async_copy(src, dst, swap_r.at[which, z]).start()

            return 0

        lax.fori_loop(0, planes, step, 0)

    def swap_land(which, seg):
        for i in range(per_segment):
            p = per_segment * seg + i
            wait(ext.at[which, pl.ds(2 * p, 2), pl.ds(STRIP, STRIP)], swap_r.at[which, p])

    def result(which, seg, go):
        def step(i, _):
            p = per_segment * seg + i
            src = results.at[which, pl.ds(2 * p, 2)]
            dst = home.at[which, :, pl.ds(pl.multiple_of(k * STRIP, STRIP), STRIP)]

            @pl.when(p != z)
            def _():
                if go:
                    start(src, dst, out_s.at[which, p], out_r.at[which, k], {"build": p, "gx": y, "gy": g})
                else:
                    wait(src, out_s.at[which, p])

            if go:

                @pl.when(p == z)
                def _():
                    pltpu.make_async_copy(src, dst, out_r.at[which, k]).start()

            return 0

        lax.fori_loop(0, per_segment, step, 0)

    def result_land(which):
        def step(n, _):
            there = pl.ds(pl.multiple_of(n * STRIP, STRIP), STRIP)
            wait(home.at[which, :, there], out_r.at[which, n])
            return 0

        lax.fori_loop(0, planes, step, 0)
        out = (pr_ref, gr_ref)[which]
        for n in range(OWN // 2):
            both = home[which, n].T
            out[2 * n] = both[0:ROWS]
            out[2 * n + 1] = both[ROWS:]

    def parts(which):
        if which == COTANGENT:
            return ((0, PAIRS // 2, STRIP // 2), (PAIRS // 2, PAIRS // 2, STRIP))
        if which == WEIGHT:
            return ((3, PAIRS - 3, STRIP),)
        return ((0, PAIRS, STRIP),)

    def columns(which, seg, go):
        for n, (first, number, width) in enumerate(parts(which)):
            pairs = pl.ds(PAIRS * seg + first, number)
            for side, ds in ((0, 1), (1, -1)):
                if side == 0:
                    here, there = pl.ds(2 * STRIP - width, width), pl.ds(STRIP - width, width)
                else:
                    here, there = pl.ds(STRIP, width), pl.ds(2 * STRIP, width)
                src, dst = ext.at[which, pairs, here], ext.at[which, pairs, there]

                @pl.when(near(ds, 0))
                def _():
                    if go:
                        start(src, dst, col_s.at[which, seg, n, side], col_r.at[which, seg, n, side],
                              owner(strip + ds, y))
                    else:
                        wait(src, col_s.at[which, seg, n, side])

    def columns_land(which, seg):
        for n, (first, number, width) in enumerate(parts(which)):
            pairs = pl.ds(PAIRS * seg + first, number)
            for side, ds in ((0, -1), (1, 1)):
                there = pl.ds(STRIP - width, width) if side == 0 else pl.ds(2 * STRIP, width)

                @pl.when(near(ds, 0))
                def _():
                    wait(ext.at[which, pairs, there], col_r.at[which, seg, n, side])

    def bands(which, seg, go):
        if go:
            for quad in range(2):
                for side in range(2):
                    packed = None
                    for m in range(4):
                        value = turned(ext[which, PAIRS * seg + 4 * quad + m], 16 * m)
                        if packed is None:
                            packed = value
                        else:
                            slot = (lane + (16 if side == 0 else 64) - 16 * m) % 64
                            packed = jnp.where(slot < 16, value, packed)
                    band_out[which, side, 2 * seg + quad] = packed
        for side, dy in ((0, 1), (1, -1)):
            src = band_out.at[which, side, pl.ds(2 * seg, 2)]
            dst = band_in.at[which, side, pl.ds(2 * seg, 2)]

            @pl.when(near(0, dy))
            def _():
                if go:
                    start(src, dst, band_s.at[which, seg, side], band_r.at[which, seg, side], owner(strip, y + dy))
                else:
                    wait(src, band_s.at[which, seg, side])

    def bands_land(which, seg):
        for side, dy in ((0, -1), (1, 1)):

            @pl.when(near(0, dy))
            def _():
                wait(band_in.at[which, side, pl.ds(2 * seg, 2)], band_r.at[which, seg, side])

    def field(which, pair, m, odd, lo, hi):
        lanes = lane[lo:hi]
        quad = pair // 4
        own = ext[which, pair, lo:hi]
        shift = -16 * m + (0 if odd else 64)
        above = turned(band_in[which, 0, quad, lo:hi], shift)
        below = turned(band_in[which, 1, quad, lo:hi], shift)
        return jnp.where(lanes < 64, turned(own, 64) if odd else own, jnp.where(lanes < 96, below, above))

    lane_own = lane[0:STRIP]

    def paired(even, odd):
        return jnp.where(lane_own < 64, even, turned(odd, 64))

    def sync(n, go):
        for ds in (-1, 0, 1):
            for dy in (-1, 0, 1):
                if ds == 0 and dy == 0:
                    continue
                src, dst = sync_out.at[n], sync_in.at[n, 1 - dy, pl.ds((1 - ds) * STRIP, STRIP)]

                @pl.when(near(ds, dy))
                def _():
                    if go:
                        start(src, dst, sync_s.at[n, 1 - dy, 1 - ds], sync_r.at[n, 1 - dy, 1 - ds],
                              owner(strip + ds, y + dy))
                    else:
                        wait(src, sync_s.at[n, 1 - dy, 1 - ds])

    def give(n, value):
        sync_out[n] = value
        sync(n, True)
        sync_in[n, 1, STRIP : 2 * STRIP] = value

    def taken(n, outside):
        for bs in range(3):
            for by in range(3):
                if bs == 1 and by == 1:
                    continue

                @pl.when(near(bs - 1, by - 1))
                def _():
                    wait(sync_in.at[n, by, pl.ds(bs * STRIP, STRIP)], sync_r.at[n, by, bs])

        above, below = turned(sync_in[n, 0], 64), turned(sync_in[n, 2], 64)
        whole = jnp.where(lane < 64, sync_in[n, 1], jnp.where(lane < 96, below, above))
        return jnp.where(inside_ref[...] > 0.5, whole, outside)

    def terms(total, des):
        bound = jnp.log2(total) * (1.0 / (LOG2_E * SHARPNESS)) - math.log(5.0) / SHARPNESS
        excess = des - bound
        under = excess * excess + SOFTNESS
        return bound, excess, under, lax.rsqrt(under)

    half = STRIP // 2
    narrow, wide = (half, REGION - half), (0, REGION)

    def own_of(v, lo):
        return v[STRIP - lo : 2 * STRIP - lo]

    def forward(seg, lo, hi, quad, w):
        mask = inside_ref[lo:hi] > 0.5
        for i in range(2):
            saved = []
            for odd in range(2):
                m = i
                pair = PAIRS * seg + 2 * quad + i
                layer = 2 * pair + odd
                des = field_dynamic(DESIGN, pair, quad, m, odd, lo, hi)
                bound, excess, under, inverse = terms(five(w), des)
                fresh = 0.5 * (des + bound - under * inverse + SOFT_ROOT)
                w = jnp.where(mask, jnp.exp2(fresh * (SHARPNESS * LOG2_E)), 1.0)
                weights[layer + 1, lo:hi] = w
                saved.append((own_of(w, lo), own_of(fresh, lo)))
            ext[WEIGHT, pair, STRIP : 2 * STRIP] = paired(saved[0][0], saved[1][0])
            results[0, pair] = paired(saved[0][1], saved[1][1])
        return w

    def field_dynamic(which, pair, part, i, odd, lo, hi):
        return field(which, pair, 2 * (part % 2) + i, odd, lo, hi)

    def forward_segment(seg, w):
        for part in range(4):
            lo, hi = wide if part < 2 else narrow
            if part == 2:
                w = w[half : REGION - half]
            w = forward(seg, lo, hi, part, w)
        return own_of(w, half)

    def fill(seg):
        bands_land(WEIGHT, seg)
        for n in range(3, PAIRS):
            for odd in range(2):
                value = field(WEIGHT, PAIRS * seg + n, n % 4, odd, 0, REGION)
                weights[DEPTH * seg + 2 * n + odd + 1] = jnp.where(inside_ref[...] > 0.5, value, 1.0)

    def prepare(seg):
        for j in range(DEPTH):
            lo, hi = narrow if j < DEPTH // 2 else wide
            layer, pair = DEPTH * seg + j, PAIRS * seg + j // 2
            total = five(weights[layer, lo:hi])
            bound, excess, under, inverse = terms(total, field(DESIGN, pair, (j // 2) % 4, j % 2, lo, hi))
            ratio = excess * inverse
            a1[layer, lo:hi] = jnp.where(inside_ref[lo:hi] > 0.5, 0.5 * (1.0 + ratio) / total, 0.0)
            a2[layer] = own_of(0.5 * (1.0 - ratio), lo)

    def backward_segment(seg, q):
        saved = None
        for j in range(DEPTH - 1, -1, -1):
            lo, hi = narrow if j < DEPTH // 2 else wide
            if j == DEPTH // 2 - 1:
                q = q[half : REGION - half]
            layer, pair = DEPTH * seg + j, PAIRS * seg + j // 2
            adjoint = field(COTANGENT, pair, (j // 2) % 4, j % 2, lo, hi) + weights[layer + 1, lo:hi] * five(q)
            q = jnp.where(inside_ref[lo:hi] > 0.5, adjoint * a1[layer, lo:hi], 0.0)
            slope = own_of(adjoint, lo) * a2[layer]
            if j % 2:
                saved = slope
            else:
                results[1, pair] = paired(slope, saved)
        return own_of(q, half)

    last = segments - 1
    swap(DESIGN, True)
    transpose_in(COTANGENT)
    swap_land(DESIGN, 0)
    columns(DESIGN, 0, True)
    columns_land(DESIGN, 0)
    bands(DESIGN, 0, True)
    swap(COTANGENT, True)
    if last > 0:
        swap_land(DESIGN, 1)
        columns(DESIGN, 1, True)
    for seg in range(segments):
        if seg == 0:
            w = jnp.where(inside_ref[...] > 0.5, math.exp(SHARPNESS), 1.0)
        else:
            w = taken(seg - 1, 1.0)
        weights[DEPTH * seg] = w
        bands_land(DESIGN, seg)
        w = forward_segment(seg, w)
        if seg < last:
            give(seg, w)
        columns(WEIGHT, seg, True)
        result(0, seg, True)
        if seg < last:
            columns_land(DESIGN, seg + 1)
            bands(DESIGN, seg + 1, True)
        if seg + 1 < last:
            swap_land(DESIGN, seg + 2)
            columns(DESIGN, seg + 2, True)
        if seg > 0:
            columns_land(WEIGHT, seg - 1)
            bands(WEIGHT, seg - 1, True)
        if seg == last - 1:
            swap_land(COTANGENT, last)
            columns(COTANGENT, last, True)

    if last == 0:
        swap_land(COTANGENT, last)
        columns(COTANGENT, last, True)
    columns_land(WEIGHT, last)
    bands(WEIGHT, last, True)
    columns_land(COTANGENT, last)
    bands(COTANGENT, last, True)
    if last > 0:
        swap_land(COTANGENT, last - 1)
        columns(COTANGENT, last - 1, True)
    fill(last)
    prepare(last)
    for seg in range(last, -1, -1):
        if seg == last:
            q = jnp.zeros((REGION, LANES), jnp.float32)
        else:
            q = taken(last + last - 1 - seg, 0.0)
        bands_land(COTANGENT, seg)
        q = backward_segment(seg, q)
        if seg > 0:
            give(last + last - seg, q)
        result(1, seg, True)
        if seg > 0:
            columns_land(COTANGENT, seg - 1)
            bands(COTANGENT, seg - 1, True)
            fill(seg - 1)
            prepare(seg - 1)
        if seg > 1:
            swap_land(COTANGENT, seg - 2)
            columns(COTANGENT, seg - 2, True)
        if seg == min(1, last):
            result_land(0)

    for which in (DESIGN, COTANGENT):
        swap(which, False)
    for seg in range(segments):
        for which in (DESIGN, COTANGENT, WEIGHT):
            columns(which, seg, False)
            bands(which, seg, False)
        for which in range(2):
            result(which, seg, False)
    for n in range(2 * last):
        sync(n, False)
    result_land(1)


def local(design, cotangent):
    shard = jax.ShapeDtypeStruct(design.shape, jnp.float32)
    planes = lax.axis_size("build")
    layers = planes * OWN
    segments = layers // DEPTH
    syncs = max(1, 2 * (segments - 1))
    f32 = lambda *shape: pltpu.VMEM(shape, jnp.float32)
    dma = lambda *shape: pltpu.SemaphoreType.DMA(shape)
    anywhere = pl.BlockSpec(memory_space=pl.ANY)
    vmem = pl.BlockSpec(memory_space=pltpu.VMEM)
    return pl.pallas_call(
        kernel,
        out_shape=(shard, shard),
        in_specs=[anywhere, anywhere],
        out_specs=(vmem, vmem),
        scratch_shapes=[
            f32(2, OWN, ROWS, planes * STRIP),
            f32(2, OWN // 2, planes * STRIP, LANES),
            f32(3, layers // 2, REGION, LANES),
            f32(3, 2, layers // 8, REGION, LANES),
            f32(3, 2, layers // 8, REGION, LANES),
            f32(layers + 1, REGION, LANES),
            f32(layers, REGION, LANES),
            f32(layers, STRIP, LANES),
            f32(2, layers // 2, STRIP, LANES),
            f32(2, OWN // 2, planes * STRIP, LANES),
            f32(syncs, STRIP, LANES),
            f32(syncs, 3, REGION, LANES),
            f32(REGION, LANES),
            dma(2),
            dma(2, planes),
            dma(2, planes),
            dma(3, segments, 2, 2),
            dma(3, segments, 2, 2),
            dma(3, segments, 2),
            dma(3, segments, 2),
            dma(syncs, 3, 3),
            dma(syncs, 3, 3),
            dma(2, planes),
            dma(2, planes),
        ],
        compiler_params=pltpu.CompilerParams(
            collective_id=0, has_side_effects=True, vmem_limit_bytes=40 * 1024 * 1024
        ),
    )(design, cotangent)


def solution(mesh):
    spec = P("build", "gx", "gy")
    return jax.shard_map(local, mesh=mesh, in_specs=(spec, spec), out_specs=(spec, spec), check_vma=False)
```

```python
import math

import jax
import jax.numpy as jnp
from jax import lax
from jax.experimental import pallas as pl
from jax.experimental.pallas import tpu as pltpu
from jax.sharding import PartitionSpec as P

MESH = pl.DeviceIdType.MESH
SHARPNESS = 40.0
SOFTNESS = 0.0001
SOFT_ROOT = 0.01
LOG2_E = 1.0 / math.log(2.0)
HALF = 0.5 * SHARPNESS * LOG2_E

OWN = 4
ROWS = 64
EDGE = 8
CHUNK = 64
STRIP = 16
REGION = 3 * STRIP
LANES = 128
DEPTH = 16
PAIRS = DEPTH // 2
DESIGN, COTANGENT, WEIGHT = range(3)


def five(v):
    cols = v.shape[0]
    by_row = pltpu.roll(v, 1, axis=1) + pltpu.roll(v, LANES - 1, axis=1)
    by_col = pltpu.roll(v, 1, axis=0) + pltpu.roll(v, cols - 1, axis=0)
    return by_row + (by_col + v)


def turned(v, shift):
    return pltpu.roll(v, shift % LANES, axis=1) if shift % LANES else v


def kernel(
    d_ref, c_ref, pr_ref, gr_ref,
    raw, nat, ext, band_out, band_in, weights, a1, sync_out, sync_in, inside_ref,
    nat_out, nat_in, border, pullbacks, nw, na1, na2, home,
    raw_sem, swap_s, swap_r, col_s, col_r, band_s, band_r, sync_s, sync_r,
    side_s, side_r, row_s, row_r, border_s, border_r, rim_s, rim_r,
):
    z, y, g = lax.axis_index("build"), lax.axis_index("gx"), lax.axis_index("gy")
    planes, xs, gys = lax.axis_size("build"), lax.axis_size("gx"), lax.axis_size("gy")
    strips = planes * gys
    width = planes * STRIP
    segments = planes * OWN // DEPTH
    per_segment = DEPTH // OWN
    last = segments - 1

    def flip(column, v):
        return v + (column % 2) * (planes - 1 - 2 * v)

    k = flip(g, z)
    strip = planes * g + k

    def owner(number, row):
        column = number // planes
        return {"build": flip(column, number % planes), "gx": row, "gy": column}

    def near(ds, dy):
        return (strip + ds >= 0) & (strip + ds < strips) & (y + dy >= 0) & (y + dy < xs)

    def start(src, dst, send, recv, dev):
        pltpu.make_async_remote_copy(
            src_ref=src, dst_ref=dst, send_sem=send, recv_sem=recv, device_id=dev, device_id_type=MESH
        ).start()

    def wait(ref, sem):
        pltpu.make_async_copy(ref, ref, sem).wait()

    for which, ref in ((DESIGN, d_ref), (COTANGENT, c_ref)):
        pltpu.make_async_copy(ref, raw.at[which], raw_sem.at[which]).start()

    barrier = pltpu.get_barrier_semaphore()
    count = jnp.int32(planes - 1)

    def greet(p, _):
        @pl.when(p != z)
        def _():
            pl.semaphore_signal(barrier, inc=1, device_id={"build": p, "gx": y, "gy": g}, device_id_type=MESH)

        return 0

    lax.fori_loop(0, planes, greet, 0)
    for ds in (-1, 0, 1):
        for dy in (-1, 0, 1):
            if ds == 0 and dy == 0:
                continue
            if dy == 0:
                valid, dev = (g + ds >= 0) & (g + ds < gys), {"build": z, "gx": y, "gy": g + ds}
            else:
                valid, dev = near(ds, dy), owner(strip + ds, y + dy)

            @pl.when(valid)
            def _():
                pl.semaphore_signal(barrier, inc=1, device_id=dev, device_id_type=MESH)

            count += jnp.where(valid, 1, 0)
    for ds in (-1, 1):
        valid = (g + ds >= 0) & (g + ds < gys)
        dev = owner(strip - k + (planes if ds == 1 else -1), y)

        @pl.when(valid & (dev["build"] != z))
        def _():
            pl.semaphore_signal(barrier, inc=1, device_id=dev, device_id_type=MESH)

        count += jnp.where(valid & (k == (planes - 1 if ds == 1 else 0)), planes - 1, 0)

    lane = lax.broadcasted_iota(jnp.int32, (REGION, LANES), 1)
    row = jnp.where(lane < 96, lane, lane - LANES) + y * ROWS
    col = lax.broadcasted_iota(jnp.int32, (REGION, LANES), 0) + (strip - 1) * STRIP
    within = (row >= 0) & (row < xs * ROWS) & (col >= 0) & (col < strips * STRIP)
    inside_ref[...] = jnp.where(within, 1.0, 0.0)

    def transpose_in(which):
        wait(raw.at[which], raw_sem.at[which])
        for n in range(OWN // 2):
            both = jnp.concatenate([raw[which, 2 * n], raw[which, 2 * n + 1]], axis=0)
            nat[which, n, EDGE : EDGE + width] = both.T

    transpose_in(DESIGN)
    pl.semaphore_wait(barrier, count)

    def swap(which, go):
        def step(i, _):
            p = (z + planes // 2 + (1 - 2 * (i % 2)) * ((i + 1) // 2) + planes) % planes
            src = nat.at[which, :, pl.ds(pl.multiple_of(EDGE + flip(g, p) * STRIP, 8), STRIP)]
            dst = ext.at[which, pl.ds(2 * z, 2), pl.ds(STRIP, STRIP)]

            @pl.when(p != z)
            def _():
                if go:
                    start(src, dst, swap_s.at[which, p], swap_r.at[which, z], {"build": p, "gx": y, "gy": g})
                else:
                    wait(src, swap_s.at[which, p])

            if go:

                @pl.when(p == z)
                def _():
                    pltpu.make_async_copy(src, dst, swap_r.at[which, z]).start()

            return 0

        lax.fori_loop(0, planes, step, 0)

    def swap_land(which, seg):
        for i in range(per_segment):
            p = per_segment * seg + i
            wait(ext.at[which, pl.ds(2 * p, 2), pl.ds(STRIP, STRIP)], swap_r.at[which, p])

    def parts(which):
        if which == COTANGENT:
            return ((0, PAIRS // 2, STRIP // 2), (PAIRS // 2, PAIRS // 2, STRIP))
        if which == WEIGHT:
            return ((3, PAIRS - 3, STRIP),)
        return ((0, PAIRS, STRIP),)

    def columns(which, seg, go):
        for n, (first, number, width) in enumerate(parts(which)):
            pairs = pl.ds(PAIRS * seg + first, number)
            for side, ds in ((0, 1), (1, -1)):
                if side == 0:
                    here, there = pl.ds(2 * STRIP - width, width), pl.ds(STRIP - width, width)
                else:
                    here, there = pl.ds(STRIP, width), pl.ds(2 * STRIP, width)
                src, dst = ext.at[which, pairs, here], ext.at[which, pairs, there]

                @pl.when(near(ds, 0))
                def _():
                    if go:
                        start(src, dst, col_s.at[which, seg, n, side], col_r.at[which, seg, n, side],
                              owner(strip + ds, y))
                    else:
                        wait(src, col_s.at[which, seg, n, side])

    def columns_land(which, seg):
        for n, (first, number, width) in enumerate(parts(which)):
            pairs = pl.ds(PAIRS * seg + first, number)
            for side, ds in ((0, -1), (1, 1)):
                there = pl.ds(STRIP - width, width) if side == 0 else pl.ds(2 * STRIP, width)

                @pl.when(near(ds, 0))
                def _():
                    wait(ext.at[which, pairs, there], col_r.at[which, seg, n, side])

    def direct(which, seg):
        return (which, seg) in ((WEIGHT, last), *((DESIGN, n) for n in range(2)))

    def spread(which, seg, ds):
        if direct(which, seg):
            return pl.ds(STRIP, STRIP), pl.ds((1 - ds) * STRIP, STRIP)
        return pl.ds(0, REGION), pl.ds(0, REGION)

    def bands(which, seg, go):
        lo, hi = (STRIP, 2 * STRIP) if direct(which, seg) else (0, REGION)
        if go:
            for quad in range(2):
                for side in range(2):
                    packed = None
                    for m in range(4):
                        value = turned(ext[which, PAIRS * seg + 4 * quad + m, lo:hi], 16 * m)
                        if packed is None:
                            packed = value
                        else:
                            slot = (lane[lo:hi] + (80 if side == 0 else 64) - 16 * m) % 64
                            packed = jnp.where(slot < 16, value, packed)
                    band_out[which, side, 2 * seg + quad, lo:hi] = packed
        for side, dy in ((0, 1), (1, -1)):
            for ds in (-1, 1, 0) if direct(which, seg) else (0,):
                here, there = spread(which, seg, ds)
                src = band_out.at[which, side, pl.ds(2 * seg, 2), here]
                dst = band_in.at[which, side, pl.ds(2 * seg, 2), there]

                @pl.when(near(ds, dy))
                def _():
                    if go:
                        start(src, dst, band_s.at[which, seg, side, 1 - ds], band_r.at[which, seg, side, 1 - ds],
                              owner(strip + ds, y + dy))
                    else:
                        wait(src, band_s.at[which, seg, side, 1 - ds])

    def bands_land(which, seg):
        for side, dy in ((0, -1), (1, 1)):
            for ds in (-1, 1, 0) if direct(which, seg) else (0,):
                _, there = spread(which, seg, ds)

                @pl.when(near(-ds, dy))
                def _():
                    wait(band_in.at[which, side, pl.ds(2 * seg, 2), there], band_r.at[which, seg, side, 1 - ds])

    def field(which, pair, m, odd, lo, hi):
        lanes = lane[lo:hi]
        quad = pair // 4
        own = ext[which, pair, lo:hi]
        shift = -16 * m + (0 if odd else 64)
        above = turned(band_in[which, 0, quad, lo:hi], shift)
        below = turned(band_in[which, 1, quad, lo:hi], shift)
        return jnp.where(lanes < 64, turned(own, 64) if odd else own, jnp.where(lanes < 96, below, above))

    lane_own = lane[0:STRIP]

    def paired(even, odd):
        return jnp.where(lane_own < 64, even, turned(odd, 64))

    def sync(n, go):
        for ds, dy in ((-1, -1), (-1, 1), (1, -1), (1, 1), (-1, 0), (1, 0), (0, -1), (0, 1)):
            src, dst = sync_out.at[n], sync_in.at[n, 1 - dy, pl.ds((1 - ds) * STRIP, STRIP)]

            @pl.when(near(ds, dy))
            def _():
                if go:
                    start(src, dst, sync_s.at[n, 1 - dy, 1 - ds], sync_r.at[n, 1 - dy, 1 - ds],
                          owner(strip + ds, y + dy))
                else:
                    wait(src, sync_s.at[n, 1 - dy, 1 - ds])

    def give(n, value):
        sync_out[n] = value
        sync(n, True)
        sync_in[n, 1, STRIP : 2 * STRIP] = value

    def taken(n, outside):
        for bs in range(3):
            for by in range(3):
                if bs == 1 and by == 1:
                    continue

                @pl.when(near(bs - 1, by - 1))
                def _():
                    wait(sync_in.at[n, by, pl.ds(bs * STRIP, STRIP)], sync_r.at[n, by, bs])

        above, below = turned(sync_in[n, 0], 64), turned(sync_in[n, 2], 64)
        whole = jnp.where(lane < 64, sync_in[n, 1], jnp.where(lane < 96, below, above))
        return jnp.where(inside_ref[...] > 0.5, whole, outside)

    def terms(total, des):
        bound = jnp.log2(total) * (1.0 / (LOG2_E * SHARPNESS)) - math.log(5.0) / SHARPNESS
        excess = des - bound
        under = excess * excess + SOFTNESS
        return bound, excess, under, lax.rsqrt(under)

    half = STRIP // 2
    narrow, wide = (half, REGION - half), (0, REGION)

    def own_of(v, lo):
        return v[STRIP - lo : 2 * STRIP - lo]

    def forward(seg, lo, hi, quad, w):
        mask = inside_ref[lo:hi] > 0.5
        for i in range(2):
            saved = []
            for odd in range(2):
                m = i
                pair = PAIRS * seg + 2 * quad + i
                layer = 2 * pair + odd
                des = field_dynamic(DESIGN, pair, quad, m, odd, lo, hi)
                level = jnp.log2(five(w))
                excess = (des + math.log(5.0) / SHARPNESS) - level * (1.0 / (LOG2_E * SHARPNESS))
                under = excess * excess + SOFTNESS
                start_of = des * HALF + (SOFT_ROOT - math.log(5.0) / SHARPNESS) * HALF
                power = (start_of + 0.5 * level) - under * lax.rsqrt(under) * HALF
                w = jnp.where(mask, jnp.exp2(power), 1.0)
                weights[layer + 1, lo:hi] = w
                saved.append(own_of(w, lo))
            ext[WEIGHT, pair, STRIP : 2 * STRIP] = paired(*saved)
        return w

    def field_dynamic(which, pair, part, i, odd, lo, hi):
        return field(which, pair, 2 * (part % 2) + i, odd, lo, hi)

    def forward_segment(seg, w):
        for part in range(4):
            lo, hi = wide if part < 2 else narrow
            if part == 2:
                w = w[half : REGION - half]
            w = forward(seg, lo, hi, part, w)
        return own_of(w, half)

    def fill(seg):
        bands_land(WEIGHT, seg)
        for n in range(3, PAIRS):
            for odd in range(2):
                if n == PAIRS - 1 and odd and seg < last:
                    continue
                value = field(WEIGHT, PAIRS * seg + n, n % 4, odd, 0, REGION)
                weights[DEPTH * seg + 2 * n + odd + 1] = jnp.where(inside_ref[...] > 0.5, value, 1.0)

    def prepare(seg):
        for j in range(DEPTH):
            lo, hi = narrow if j < DEPTH // 2 else wide
            layer, pair = DEPTH * seg + j, PAIRS * seg + j // 2
            total = five(weights[layer, lo:hi])
            bound, excess, under, inverse = terms(total, field(DESIGN, pair, (j // 2) % 4, j % 2, lo, hi))
            ratio = excess * inverse
            a1[layer, lo:hi] = jnp.where(inside_ref[lo:hi] > 0.5, 0.5 * (1.0 + ratio) / total, 0.0)

    def backward_segment(seg, q):
        for j in range(DEPTH - 1, OWN - 1 if seg == 0 else -1, -1):
            lo, hi = narrow if j < DEPTH // 2 else wide
            if j == DEPTH // 2 - 1:
                q = q[half : REGION - half]
            layer, pair = DEPTH * seg + j, PAIRS * seg + j // 2
            adjoint = field(COTANGENT, pair, (j // 2) % 4, j % 2, lo, hi) + weights[layer + 1, lo:hi] * five(q)
            q = jnp.where(inside_ref[lo:hi] > 0.5, adjoint * a1[layer, lo:hi], 0.0)
            if j % OWN == 0 and j > 0:
                pullbacks[layer // OWN - 1] = own_of(q, lo)
        return own_of(q, half)

    on_right = k > 0
    onward = jnp.where(on_right, g + 1, g - 1)
    outermost = ((k == 0) & (g > 0)) | ((k == planes - 1) & (g < gys - 1))

    def piece(kind, p, go):
        def source(first, number):
            first = pl.multiple_of(first, 8)
            if kind == 0:
                return weights.at[OWN * p, pl.ds(pl.multiple_of(STRIP + first, 8), number)]
            return pullbacks.at[p, pl.ds(first, number)]

        src = source(0, STRIP)
        dst = border.at[kind, pl.ds(pl.multiple_of(EDGE + k * STRIP, 8), STRIP)]

        @pl.when(p != z)
        def _():
            if go:
                start(src, dst, border_s.at[kind, p], border_r.at[kind, k], {"build": p, "gx": y, "gy": g})
            else:
                wait(src, border_s.at[kind, p])

        if go:

            @pl.when(p == z)
            def _():
                pltpu.make_async_copy(src, dst, border_r.at[kind, k]).start()

        rim = source(jnp.where(on_right, STRIP - EDGE, 0), EDGE)
        there = border.at[kind, pl.ds(pl.multiple_of(jnp.where(on_right, 0, EDGE + width), 8), EDGE)]

        @pl.when(outermost)
        def _():
            if go:
                start(rim, there, rim_s.at[kind, p], rim_r.at[kind, jnp.where(on_right, 0, 1)],
                      {"build": p, "gx": y, "gy": onward})
            else:
                wait(rim, rim_s.at[kind, p])

    def lift(seg):
        for p in range(per_segment * seg, min(per_segment * (seg + 1), planes - 1)):
            piece(1, p, True)

    def support(seg):
        for p in range(max(1, per_segment * seg), per_segment * (seg + 1)):
            piece(0, p, True)

    def present(kind):
        return z > 0 if kind == 0 else z < planes - 1

    def border_land(kind):
        @pl.when(present(kind))
        def _():
            def step(n, _):
                wait(border.at[kind, pl.ds(pl.multiple_of(EDGE + n * STRIP, 8), STRIP)], border_r.at[kind, n])
                return 0

            lax.fori_loop(0, planes, step, 0)

        for side, there, valid in ((0, 0, g > 0), (1, EDGE + width, g < gys - 1)):

            @pl.when(valid & present(kind))
            def _():
                wait(border.at[kind, pl.ds(there, EDGE)], rim_r.at[kind, side])

    def beside(side):
        dg = 1 - 2 * side
        here = pl.ds(width, EDGE) if side == 0 else pl.ds(EDGE, EDGE)
        there = pl.ds(0, EDGE) if side == 0 else pl.ds(EDGE + width, EDGE)
        return here, there, (g + dg >= 0) & (g + dg < gys), {"build": z, "gx": y, "gy": g + dg}

    def sides(which, go):
        for side in range(2):
            here, there, valid, dev = beside(side)
            src, dst = nat.at[which, :, here], nat.at[which, :, there]

            @pl.when(valid)
            def _():
                if go:
                    start(src, dst, side_s.at[which, side], side_r.at[which, side], dev)
                else:
                    wait(src, side_s.at[which, side])

    def sides_land(which):
        for side in range(2):
            _, there, _, _ = beside(side)
            _, _, valid, _ = beside(1 - side)

            @pl.when(valid)
            def _():
                wait(nat.at[which, :, there], side_r.at[which, side])

    lane_nat = lax.broadcasted_iota(jnp.int32, (width + 2 * EDGE, LANES), 1)

    def rows(go):
        for side, dy in ((0, 1), (1, -1)):
            if go:
                packed = nat[DESIGN, 0]
                for m in range(1, OWN):
                    slot = (lane_nat + (80 if side == 0 else 64) - 16 * m) % 64
                    packed = jnp.where(slot < 16, turned(nat[m // 2, m % 2], 16 * m), packed)
                nat_out[side] = packed

            @pl.when((y + dy >= 0) & (y + dy < xs))
            def _():
                dev = {"build": z, "gx": y + dy, "gy": g}
                if go:
                    start(nat_out.at[side], nat_in.at[side], row_s.at[side], row_r.at[side], dev)
                else:
                    wait(nat_out.at[side], row_s.at[side])

    def rows_land():
        for side, dy in ((0, -1), (1, 1)):

            @pl.when((y + dy >= 0) & (y + dy < xs))
            def _():
                wait(nat_in.at[side], row_r.at[side])

    reach = CHUNK + 2 * EDGE
    lane_reach = lax.broadcasted_iota(jnp.int32, (reach, LANES), 1)

    def own_field(which, j, span):
        own = nat[which, j // 2, span]
        shift = -16 * (2 * which + j // 2) + (0 if j % 2 else 64)
        above = turned(nat_in[0, span], shift)
        below = turned(nat_in[1, span], shift)
        own = turned(own, 64) if j % 2 else own
        return jnp.where(lane_reach < 64, own, jnp.where(lane_reach < 96, below, above))

    def chunk_mask(c):
        at_row = jnp.where(lane_reach < 96, lane_reach, lane_reach - LANES) + y * ROWS
        at_col = lax.broadcasted_iota(jnp.int32, (reach, LANES), 0) + (width * g + CHUNK * c - EDGE)
        return (at_row >= 0) & (at_row < xs * ROWS) & (at_col >= 0) & (at_col < gys * width)

    def both_layers(even, odd):
        return jnp.where(lane_reach[0:CHUNK] < 64, even, turned(odd, 64))

    def own_forward(c, _):
        span = pl.ds(pl.multiple_of(CHUNK * c, CHUNK), reach)
        mask = chunk_mask(c)
        w = jnp.where(z == 0, math.exp(SHARPNESS), border[0, span])
        w = jnp.where(mask, w, 1.0)
        saved = None
        for j in range(OWN):
            des = own_field(DESIGN, j, span)
            total = five(w)
            bound, excess, under, inverse = terms(total, des)
            ratio = excess * inverse
            na1[c, j] = jnp.where(mask, 0.5 * (1.0 + ratio) / total, 0.0)
            na2[c, j] = 0.5 * (1.0 - ratio[EDGE : EDGE + CHUNK])
            fresh = 0.5 * (des + bound - under * inverse + SOFT_ROOT)
            w = jnp.where(mask, jnp.exp2(fresh * (SHARPNESS * LOG2_E)), 1.0)
            nw[c, j] = w
            mine = fresh[EDGE : EDGE + CHUNK]
            if j % 2:
                home[0, j // 2, pl.ds(pl.multiple_of(CHUNK * c, CHUNK), CHUNK)] = both_layers(saved, mine)
            saved = mine
        return 0

    def own_backward(c, _):
        span = pl.ds(pl.multiple_of(CHUNK * c, CHUNK), reach)
        mask = chunk_mask(c)
        q = jnp.where(mask & present(1), border[1, span], 0.0)
        saved = None
        for j in range(OWN - 1, -1, -1):
            adjoint = own_field(COTANGENT, j, span) + nw[c, j] * five(q)
            q = jnp.where(mask, adjoint * na1[c, j], 0.0)
            mine = adjoint[EDGE : EDGE + CHUNK] * na2[c, j]
            if j % 2 == 0:
                home[1, j // 2, pl.ds(pl.multiple_of(CHUNK * c, CHUNK), CHUNK)] = both_layers(mine, saved)
            saved = mine
        return 0

    def put(which):
        out = (pr_ref, gr_ref)[which]
        for n in range(OWN // 2):
            both = home[which, n].T
            out[2 * n] = both[0:ROWS]
            out[2 * n + 1] = both[ROWS:]

    swap(DESIGN, True)
    transpose_in(COTANGENT)
    for which in (DESIGN, COTANGENT):
        sides(which, True)
    for which in (DESIGN, COTANGENT):
        sides_land(which)
    rows(True)
    swap_land(DESIGN, 0)
    bands(DESIGN, 0, True)
    columns(DESIGN, 0, True)
    swap(COTANGENT, True)
    if last > 0:
        swap_land(DESIGN, 1)
        if direct(DESIGN, 1):
            bands(DESIGN, 1, True)
        columns(DESIGN, 1, True)
    for seg in range(segments):
        if seg == 0:
            w = jnp.where(inside_ref[...] > 0.5, math.exp(SHARPNESS), 1.0)
        else:
            w = taken(seg - 1, 1.0)
        weights[DEPTH * seg] = w
        if direct(DESIGN, seg):
            columns_land(DESIGN, seg)
        bands_land(DESIGN, seg)
        w = forward_segment(seg, w)
        if seg < last:
            give(seg, w)
        if seg == last:
            bands(WEIGHT, seg, True)
        columns(WEIGHT, seg, True)
        if seg < last:
            if not direct(DESIGN, seg + 1):
                columns_land(DESIGN, seg + 1)
                bands(DESIGN, seg + 1, True)
        if seg + 1 < last:
            swap_land(DESIGN, seg + 2)
            if direct(DESIGN, seg + 2):
                bands(DESIGN, seg + 2, True)
            columns(DESIGN, seg + 2, True)
        if seg > 0:
            columns_land(WEIGHT, seg - 1)
            bands(WEIGHT, seg - 1, True)
        if seg > 1:
            fill(seg - 2)
            support(seg - 2)
        if seg == max(0, last - 2):
            swap_land(COTANGENT, last)
            columns(COTANGENT, last, True)
        if seg == max(0, last - 1):
            columns_land(COTANGENT, last)
            bands(COTANGENT, last, True)
            if last > 0:
                swap_land(COTANGENT, last - 1)
                columns(COTANGENT, last - 1, True)

    if last > 0:
        columns_land(COTANGENT, last - 1)
        bands(COTANGENT, last - 1, True)
    if last > 1:
        swap_land(COTANGENT, last - 2)
        columns(COTANGENT, last - 2, True)
    if last > 0:
        fill(last - 1)
        prepare(last - 1)
    columns_land(WEIGHT, last)
    fill(last)
    prepare(last)
    for seg in range(last, -1, -1):
        if seg == last:
            q = jnp.zeros((REGION, LANES), jnp.float32)
        else:
            q = taken(last + last - 1 - seg, 0.0)
            pullbacks[per_segment * (seg + 1) - 1] = own_of(q, 0)
        bands_land(COTANGENT, seg)
        q = backward_segment(seg, q)
        if seg > 0:
            give(last + last - seg, q)
        lift(seg)
        if seg > 1:
            columns_land(COTANGENT, seg - 2)
            bands(COTANGENT, seg - 2, True)
        if seg > 2:
            swap_land(COTANGENT, seg - 3)
            columns(COTANGENT, seg - 3, True)
        if seg > 1:
            prepare(seg - 2)
        if seg == last:
            for other in range(max(0, last - 1), last + 1):
                support(other)
    rows_land()
    border_land(0)
    lax.fori_loop(0, width // CHUNK, own_forward, 0)
    put(0)

    for which in (DESIGN, COTANGENT):
        swap(which, False)
        sides(which, False)
    for seg in range(segments):
        for which in (DESIGN, COTANGENT, WEIGHT):
            columns(which, seg, False)
            bands(which, seg, False)
    for n in range(2 * last):
        sync(n, False)
    rows(False)
    for p in range(1, planes):
        piece(0, p, False)
    for p in range(per_segment, planes - 1):
        piece(1, p, False)

    border_land(1)
    lax.fori_loop(0, width // CHUNK, own_backward, 0)
    put(1)
    for p in range(min(per_segment, planes - 1)):
        piece(1, p, False)


def local(design, cotangent):
    shard = jax.ShapeDtypeStruct(design.shape, jnp.float32)
    planes = lax.axis_size("build")
    layers = planes * OWN
    segments = layers // DEPTH
    width = planes * STRIP
    chunks = width // CHUNK
    syncs = max(1, 2 * (segments - 1))
    f32 = lambda *shape: pltpu.VMEM(shape, jnp.float32)
    dma = lambda *shape: pltpu.SemaphoreType.DMA(shape)
    anywhere = pl.BlockSpec(memory_space=pl.ANY)
    vmem = pl.BlockSpec(memory_space=pltpu.VMEM)
    return pl.pallas_call(
        kernel,
        out_shape=(shard, shard),
        in_specs=[anywhere, anywhere],
        out_specs=(vmem, vmem),
        scratch_shapes=[
            f32(2, OWN, ROWS, width),
            f32(2, OWN // 2, width + 2 * EDGE, LANES),
            f32(3, layers // 2, REGION, LANES),
            f32(3, 2, layers // 8, REGION, LANES),
            f32(3, 2, layers // 8, REGION, LANES),
            f32(layers + 1, REGION, LANES),
            f32(layers, REGION, LANES),
            f32(syncs, STRIP, LANES),
            f32(syncs, 3, REGION, LANES),
            f32(REGION, LANES),
            f32(2, width + 2 * EDGE, LANES),
            f32(2, width + 2 * EDGE, LANES),
            f32(2, width + 2 * EDGE, LANES),
            f32(planes, STRIP, LANES),
            f32(chunks, OWN, CHUNK + 2 * EDGE, LANES),
            f32(chunks, OWN, CHUNK + 2 * EDGE, LANES),
            f32(chunks, OWN, CHUNK, LANES),
            f32(2, OWN // 2, width, LANES),
            dma(2),
            dma(2, planes),
            dma(2, planes),
            dma(3, segments, 2, 2),
            dma(3, segments, 2, 2),
            dma(3, segments, 2, 3),
            dma(3, segments, 2, 3),
            dma(syncs, 3, 3),
            dma(syncs, 3, 3),
            dma(2, 2),
            dma(2, 2),
            dma(2),
            dma(2),
            dma(2, planes),
            dma(2, planes),
            dma(2, planes),
            dma(2, 2),
        ],
        compiler_params=pltpu.CompilerParams(
            collective_id=0, has_side_effects=True, vmem_limit_bytes=40 * 1024 * 1024
        ),
    )(design, cotangent)


def solution(mesh):
    spec = P("build", "gx", "gy")
    return jax.shard_map(local, mesh=mesh, in_specs=(spec, spec), out_specs=(spec, spec), check_vma=False)
```

```python
import math

import jax
import jax.numpy as jnp
from jax import lax
from jax.experimental import pallas as pl
from jax.experimental.pallas import tpu as pltpu
from jax.sharding import PartitionSpec as P

MESH = pl.DeviceIdType.MESH
SHARPNESS = 40.0
SOFTNESS = 0.0001
SOFT_ROOT = 0.01
LOG2_E = 1.0 / math.log(2.0)
HALF = 0.5 * SHARPNESS * LOG2_E

OWN = 4
ROWS = 64
EDGE = 8
CHUNK = 64
STRIP = 16
REGION = 3 * STRIP
LANES = 128
DEPTH = 16
PAIRS = DEPTH // 2
DESIGN, COTANGENT, WEIGHT = range(3)


def five(v):
    cols = v.shape[0]
    by_row = pltpu.roll(v, 1, axis=1) + pltpu.roll(v, LANES - 1, axis=1)
    by_col = pltpu.roll(v, 1, axis=0) + pltpu.roll(v, cols - 1, axis=0)
    return by_row + (by_col + v)


def turned(v, shift):
    return pltpu.roll(v, shift % LANES, axis=1) if shift % LANES else v


def kernel(
    d_ref, c_ref, pr_ref, gr_ref,
    raw, nat, ext, band_out, band_in, weights, a1, sync_out, sync_in, inside_ref,
    nat_out, nat_in, border, pullbacks, nw, na1, na2, home,
    raw_sem, swap_s, swap_r, col_s, col_r, band_s, band_r, sync_s, sync_r,
    side_s, side_r, row_s, row_r, border_s, border_r, rim_s, rim_r,
):
    z, y, g = lax.axis_index("build"), lax.axis_index("gx"), lax.axis_index("gy")
    planes, xs, gys = lax.axis_size("build"), lax.axis_size("gx"), lax.axis_size("gy")
    strips = planes * gys
    width = planes * STRIP
    segments = planes * OWN // DEPTH
    per_segment = DEPTH // OWN
    last = segments - 1

    def flip(column, v):
        return v + (column % 2) * (planes - 1 - 2 * v)

    k = flip(g, z)
    strip = planes * g + k

    def owner(number, row):
        column = number // planes
        return {"build": flip(column, number % planes), "gx": row, "gy": column}

    def near(ds, dy):
        return (strip + ds >= 0) & (strip + ds < strips) & (y + dy >= 0) & (y + dy < xs)

    def start(src, dst, send, recv, dev):
        pltpu.make_async_remote_copy(
            src_ref=src, dst_ref=dst, send_sem=send, recv_sem=recv, device_id=dev, device_id_type=MESH
        ).start()

    def wait(ref, sem):
        pltpu.make_async_copy(ref, ref, sem).wait()

    for which, ref in ((DESIGN, d_ref), (COTANGENT, c_ref)):
        pltpu.make_async_copy(ref, raw.at[which], raw_sem.at[which]).start()

    barrier = pltpu.get_barrier_semaphore()
    count = jnp.int32(planes - 1)

    def greet(p, _):
        @pl.when(p != z)
        def _():
            pl.semaphore_signal(barrier, inc=1, device_id={"build": p, "gx": y, "gy": g}, device_id_type=MESH)

        return 0

    lax.fori_loop(0, planes, greet, 0)
    for ds in (-1, 0, 1):
        for dy in (-1, 0, 1):
            if ds == 0 and dy == 0:
                continue
            if dy == 0:
                valid, dev = (g + ds >= 0) & (g + ds < gys), {"build": z, "gx": y, "gy": g + ds}
            else:
                valid, dev = near(ds, dy), owner(strip + ds, y + dy)

            @pl.when(valid)
            def _():
                pl.semaphore_signal(barrier, inc=1, device_id=dev, device_id_type=MESH)

            count += jnp.where(valid, 1, 0)
    for ds in (-1, 1):
        valid = (g + ds >= 0) & (g + ds < gys)
        dev = owner(strip - k + (planes if ds == 1 else -1), y)

        @pl.when(valid & (dev["build"] != z))
        def _():
            pl.semaphore_signal(barrier, inc=1, device_id=dev, device_id_type=MESH)

        count += jnp.where(valid & (k == (planes - 1 if ds == 1 else 0)), planes - 1, 0)

    lane = lax.broadcasted_iota(jnp.int32, (REGION, LANES), 1)
    row = jnp.where(lane < 96, lane, lane - LANES) + y * ROWS
    col = lax.broadcasted_iota(jnp.int32, (REGION, LANES), 0) + (strip - 1) * STRIP
    within = (row >= 0) & (row < xs * ROWS) & (col >= 0) & (col < strips * STRIP)
    inside_ref[...] = jnp.where(within, 1.0, 0.0)

    def transpose_in(which):
        wait(raw.at[which], raw_sem.at[which])
        for n in range(OWN // 2):
            both = jnp.concatenate([raw[which, 2 * n], raw[which, 2 * n + 1]], axis=0)
            nat[which, n, EDGE : EDGE + width] = both.T

    transpose_in(DESIGN)
    pl.semaphore_wait(barrier, count)

    def swap(which, go):
        def step(i, _):
            p = (z + planes // 2 + (1 - 2 * (i % 2)) * ((i + 1) // 2) + planes) % planes
            src = nat.at[which, :, pl.ds(pl.multiple_of(EDGE + flip(g, p) * STRIP, 8), STRIP)]
            dst = ext.at[which, pl.ds(2 * z, 2), pl.ds(STRIP, STRIP)]

            @pl.when(p != z)
            def _():
                if go:
                    start(src, dst, swap_s.at[which, p], swap_r.at[which, z], {"build": p, "gx": y, "gy": g})
                else:
                    wait(src, swap_s.at[which, p])

            if go:

                @pl.when(p == z)
                def _():
                    pltpu.make_async_copy(src, dst, swap_r.at[which, z]).start()

            return 0

        lax.fori_loop(0, planes, step, 0)

    def swap_land(which, seg):
        for i in range(per_segment):
            p = per_segment * seg + i
            wait(ext.at[which, pl.ds(2 * p, 2), pl.ds(STRIP, STRIP)], swap_r.at[which, p])

    def parts(which):
        if which == COTANGENT:
            return ((0, PAIRS // 2, STRIP // 2), (PAIRS // 2, PAIRS // 2, STRIP))
        if which == WEIGHT:
            return ((3, PAIRS - 3, STRIP),)
        return ((0, PAIRS, STRIP),)

    def columns(which, seg, go):
        for n, (first, number, width) in enumerate(parts(which)):
            pairs = pl.ds(PAIRS * seg + first, number)
            for side, ds in ((0, 1), (1, -1)):
                if side == 0:
                    here, there = pl.ds(2 * STRIP - width, width), pl.ds(STRIP - width, width)
                else:
                    here, there = pl.ds(STRIP, width), pl.ds(2 * STRIP, width)
                src, dst = ext.at[which, pairs, here], ext.at[which, pairs, there]

                @pl.when(near(ds, 0))
                def _():
                    if go:
                        start(src, dst, col_s.at[which, seg, n, side], col_r.at[which, seg, n, side],
                              owner(strip + ds, y))
                    else:
                        wait(src, col_s.at[which, seg, n, side])

    def columns_land(which, seg):
        for n, (first, number, width) in enumerate(parts(which)):
            pairs = pl.ds(PAIRS * seg + first, number)
            for side, ds in ((0, -1), (1, 1)):
                there = pl.ds(STRIP - width, width) if side == 0 else pl.ds(2 * STRIP, width)

                @pl.when(near(ds, 0))
                def _():
                    wait(ext.at[which, pairs, there], col_r.at[which, seg, n, side])

    def direct(which, seg):
        return (which, seg) in ((WEIGHT, last), *((DESIGN, n) for n in range(2)))

    def spread(which, seg, ds):
        if direct(which, seg):
            return pl.ds(STRIP, STRIP), pl.ds((1 - ds) * STRIP, STRIP)
        return pl.ds(0, REGION), pl.ds(0, REGION)

    def bands(which, seg, go):
        lo, hi = (STRIP, 2 * STRIP) if direct(which, seg) else (0, REGION)
        if go:
            for quad in range(2):
                for side in range(2):
                    packed = None
                    for m in range(4):
                        value = turned(ext[which, PAIRS * seg + 4 * quad + m, lo:hi], 16 * m)
                        if packed is None:
                            packed = value
                        else:
                            slot = (lane[lo:hi] + (80 if side == 0 else 64) - 16 * m) % 64
                            packed = jnp.where(slot < 16, value, packed)
                    band_out[which, side, 2 * seg + quad, lo:hi] = packed
        for side, dy in ((0, 1), (1, -1)):
            for ds in (-1, 1, 0) if direct(which, seg) else (0,):
                here, there = spread(which, seg, ds)
                src = band_out.at[which, side, pl.ds(2 * seg, 2), here]
                dst = band_in.at[which, side, pl.ds(2 * seg, 2), there]

                @pl.when(near(ds, dy))
                def _():
                    if go:
                        start(src, dst, band_s.at[which, seg, side, 1 - ds], band_r.at[which, seg, side, 1 - ds],
                              owner(strip + ds, y + dy))
                    else:
                        wait(src, band_s.at[which, seg, side, 1 - ds])

    def bands_land(which, seg):
        for side, dy in ((0, -1), (1, 1)):
            for ds in (-1, 1, 0) if direct(which, seg) else (0,):
                _, there = spread(which, seg, ds)

                @pl.when(near(-ds, dy))
                def _():
                    wait(band_in.at[which, side, pl.ds(2 * seg, 2), there], band_r.at[which, seg, side, 1 - ds])

    def field(which, pair, m, odd, lo, hi):
        lanes = lane[lo:hi]
        quad = pair // 4
        own = ext[which, pair, lo:hi]
        shift = -16 * m + (0 if odd else 64)
        above = turned(band_in[which, 0, quad, lo:hi], shift)
        below = turned(band_in[which, 1, quad, lo:hi], shift)
        return jnp.where(lanes < 64, turned(own, 64) if odd else own, jnp.where(lanes < 96, below, above))

    lane_own = lane[0:STRIP]

    def paired(even, odd):
        return jnp.where(lane_own < 64, even, turned(odd, 64))

    def sync(n, go):
        for ds, dy in ((-1, -1), (-1, 1), (1, -1), (1, 1), (-1, 0), (1, 0), (0, -1), (0, 1)):
            src, dst = sync_out.at[n], sync_in.at[n, 1 - dy, pl.ds((1 - ds) * STRIP, STRIP)]

            @pl.when(near(ds, dy))
            def _():
                if go:
                    start(src, dst, sync_s.at[n, 1 - dy, 1 - ds], sync_r.at[n, 1 - dy, 1 - ds],
                          owner(strip + ds, y + dy))
                else:
                    wait(src, sync_s.at[n, 1 - dy, 1 - ds])

    def give(n, value):
        sync_out[n] = value
        sync(n, True)
        sync_in[n, 1, STRIP : 2 * STRIP] = value

    def taken(n, outside):
        for bs in range(3):
            for by in range(3):
                if bs == 1 and by == 1:
                    continue

                @pl.when(near(bs - 1, by - 1))
                def _():
                    wait(sync_in.at[n, by, pl.ds(bs * STRIP, STRIP)], sync_r.at[n, by, bs])

        above, below = turned(sync_in[n, 0], 64), turned(sync_in[n, 2], 64)
        whole = jnp.where(lane < 64, sync_in[n, 1], jnp.where(lane < 96, below, above))
        return jnp.where(inside_ref[...] > 0.5, whole, outside)

    def terms(total, des):
        bound = jnp.log2(total) * (1.0 / (LOG2_E * SHARPNESS)) - math.log(5.0) / SHARPNESS
        excess = des - bound
        under = excess * excess + SOFTNESS
        return bound, excess, under, lax.rsqrt(under)

    half = STRIP // 2
    narrow, wide = (half, REGION - half), (0, REGION)

    def own_of(v, lo):
        return v[STRIP - lo : 2 * STRIP - lo]

    def forward(seg, lo, hi, quad, w):
        mask = inside_ref[lo:hi] > 0.5
        for i in range(2):
            saved = []
            for odd in range(2):
                m = i
                pair = PAIRS * seg + 2 * quad + i
                layer = 2 * pair + odd
                des = field_dynamic(DESIGN, pair, quad, m, odd, lo, hi)
                level = jnp.log2(five(w))
                excess = (des + math.log(5.0) / SHARPNESS) - level * (1.0 / (LOG2_E * SHARPNESS))
                under = excess * excess + SOFTNESS
                start_of = des * HALF + (SOFT_ROOT - math.log(5.0) / SHARPNESS) * HALF
                power = (start_of + 0.5 * level) - under * lax.rsqrt(under) * HALF
                w = jnp.where(mask, jnp.exp2(power), 1.0)
                weights[layer + 1, lo:hi] = w
                saved.append(own_of(w, lo))
            ext[WEIGHT, pair, STRIP : 2 * STRIP] = paired(*saved)
        return w

    def field_dynamic(which, pair, part, i, odd, lo, hi):
        return field(which, pair, 2 * (part % 2) + i, odd, lo, hi)

    def forward_segment(seg, w):
        for part in range(4):
            lo, hi = wide if part < 2 else narrow
            if part == 2:
                w = w[half : REGION - half]
            w = forward(seg, lo, hi, part, w)
        return own_of(w, half)

    def fill(seg):
        bands_land(WEIGHT, seg)
        for n in range(3, PAIRS):
            for odd in range(2):
                if n == PAIRS - 1 and odd and seg < last:
                    continue
                value = field(WEIGHT, PAIRS * seg + n, n % 4, odd, 0, REGION)
                weights[DEPTH * seg + 2 * n + odd + 1] = jnp.where(inside_ref[...] > 0.5, value, 1.0)

    def prepare(seg):
        for j in range(DEPTH):
            lo, hi = narrow if j < DEPTH // 2 else wide
            layer, pair = DEPTH * seg + j, PAIRS * seg + j // 2
            total = five(weights[layer, lo:hi])
            bound, excess, under, inverse = terms(total, field(DESIGN, pair, (j // 2) % 4, j % 2, lo, hi))
            ratio = excess * inverse
            a1[layer, lo:hi] = jnp.where(inside_ref[lo:hi] > 0.5, 0.5 * (1.0 + ratio) / total, 0.0)

    def backward_segment(seg, q):
        for j in range(DEPTH - 1, OWN - 1 if seg == 0 else -1, -1):
            lo, hi = narrow if j < DEPTH // 2 else wide
            if j == DEPTH // 2 - 1:
                q = q[half : REGION - half]
            layer, pair = DEPTH * seg + j, PAIRS * seg + j // 2
            adjoint = field(COTANGENT, pair, (j // 2) % 4, j % 2, lo, hi) + weights[layer + 1, lo:hi] * five(q)
            q = jnp.where(inside_ref[lo:hi] > 0.5, adjoint * a1[layer, lo:hi], 0.0)
            if j % OWN == 0 and j > 0:
                pullbacks[layer // OWN - 1] = own_of(q, lo)
        return own_of(q, half)

    on_right = k > 0
    onward = jnp.where(on_right, g + 1, g - 1)
    outermost = ((k == 0) & (g > 0)) | ((k == planes - 1) & (g < gys - 1))

    def piece(kind, p, go):
        def source(first, number):
            first = pl.multiple_of(first, 8)
            if kind == 0:
                return weights.at[OWN * p, pl.ds(pl.multiple_of(STRIP + first, 8), number)]
            return pullbacks.at[p, pl.ds(first, number)]

        src = source(0, STRIP)
        dst = border.at[kind, pl.ds(pl.multiple_of(EDGE + k * STRIP, 8), STRIP)]

        @pl.when(p != z)
        def _():
            if go:
                start(src, dst, border_s.at[kind, p], border_r.at[kind, k], {"build": p, "gx": y, "gy": g})
            else:
                wait(src, border_s.at[kind, p])

        if go:

            @pl.when(p == z)
            def _():
                pltpu.make_async_copy(src, dst, border_r.at[kind, k]).start()

        rim = source(jnp.where(on_right, STRIP - EDGE, 0), EDGE)
        there = border.at[kind, pl.ds(pl.multiple_of(jnp.where(on_right, 0, EDGE + width), 8), EDGE)]

        @pl.when(outermost)
        def _():
            if go:
                start(rim, there, rim_s.at[kind, p], rim_r.at[kind, jnp.where(on_right, 0, 1)],
                      {"build": p, "gx": y, "gy": onward})
            else:
                wait(rim, rim_s.at[kind, p])

    def lift(seg):
        for p in range(per_segment * seg, min(per_segment * (seg + 1), planes - 1)):
            piece(1, p, True)

    def support(seg):
        for p in range(max(1, per_segment * seg), per_segment * (seg + 1)):
            piece(0, p, True)

    def present(kind):
        return z > 0 if kind == 0 else z < planes - 1

    def border_land(kind):
        @pl.when(present(kind))
        def _():
            def step(n, _):
                wait(border.at[kind, pl.ds(pl.multiple_of(EDGE + n * STRIP, 8), STRIP)], border_r.at[kind, n])
                return 0

            lax.fori_loop(0, planes, step, 0)

        for side, there, valid in ((0, 0, g > 0), (1, EDGE + width, g < gys - 1)):

            @pl.when(valid & present(kind))
            def _():
                wait(border.at[kind, pl.ds(there, EDGE)], rim_r.at[kind, side])

    def beside(side):
        dg = 1 - 2 * side
        here = pl.ds(width, EDGE) if side == 0 else pl.ds(EDGE, EDGE)
        there = pl.ds(0, EDGE) if side == 0 else pl.ds(EDGE + width, EDGE)
        return here, there, (g + dg >= 0) & (g + dg < gys), {"build": z, "gx": y, "gy": g + dg}

    def sides(which, go):
        for side in range(2):
            here, there, valid, dev = beside(side)
            src, dst = nat.at[which, :, here], nat.at[which, :, there]

            @pl.when(valid)
            def _():
                if go:
                    start(src, dst, side_s.at[which, side], side_r.at[which, side], dev)
                else:
                    wait(src, side_s.at[which, side])

    def sides_land(which):
        for side in range(2):
            _, there, _, _ = beside(side)
            _, _, valid, _ = beside(1 - side)

            @pl.when(valid)
            def _():
                wait(nat.at[which, :, there], side_r.at[which, side])

    lane_nat = lax.broadcasted_iota(jnp.int32, (width + 2 * EDGE, LANES), 1)

    def rows(go):
        for side, dy in ((0, 1), (1, -1)):
            if go:
                packed = nat[DESIGN, 0]
                for m in range(1, OWN):
                    slot = (lane_nat + (80 if side == 0 else 64) - 16 * m) % 64
                    packed = jnp.where(slot < 16, turned(nat[m // 2, m % 2], 16 * m), packed)
                nat_out[side] = packed

            @pl.when((y + dy >= 0) & (y + dy < xs))
            def _():
                dev = {"build": z, "gx": y + dy, "gy": g}
                if go:
                    start(nat_out.at[side], nat_in.at[side], row_s.at[side], row_r.at[side], dev)
                else:
                    wait(nat_out.at[side], row_s.at[side])

    def rows_land():
        for side, dy in ((0, -1), (1, 1)):

            @pl.when((y + dy >= 0) & (y + dy < xs))
            def _():
                wait(nat_in.at[side], row_r.at[side])

    reach = CHUNK + 2 * EDGE
    lane_reach = lax.broadcasted_iota(jnp.int32, (reach, LANES), 1)

    def own_field(which, j, span):
        own = nat[which, j // 2, span]
        shift = -16 * (2 * which + j // 2) + (0 if j % 2 else 64)
        above = turned(nat_in[0, span], shift)
        below = turned(nat_in[1, span], shift)
        own = turned(own, 64) if j % 2 else own
        return jnp.where(lane_reach < 64, own, jnp.where(lane_reach < 96, below, above))

    def chunk_mask(c):
        at_row = jnp.where(lane_reach < 96, lane_reach, lane_reach - LANES) + y * ROWS
        at_col = lax.broadcasted_iota(jnp.int32, (reach, LANES), 0) + (width * g + CHUNK * c - EDGE)
        return (at_row >= 0) & (at_row < xs * ROWS) & (at_col >= 0) & (at_col < gys * width)

    def both_layers(even, odd):
        return jnp.where(lane_reach[0:CHUNK] < 64, even, turned(odd, 64))

    def own_forward(c, _):
        span = pl.ds(pl.multiple_of(CHUNK * c, CHUNK), reach)
        mask = chunk_mask(c)
        w = jnp.where(z == 0, math.exp(SHARPNESS), border[0, span])
        w = jnp.where(mask, w, 1.0)
        saved = None
        for j in range(OWN):
            des = own_field(DESIGN, j, span)
            total = five(w)
            bound, excess, under, inverse = terms(total, des)
            ratio = excess * inverse
            na1[c, j] = jnp.where(mask, 0.5 * (1.0 + ratio) / total, 0.0)
            na2[c, j] = 0.5 * (1.0 - ratio[EDGE : EDGE + CHUNK])
            fresh = 0.5 * (des + bound - under * inverse + SOFT_ROOT)
            w = jnp.where(mask, jnp.exp2(fresh * (SHARPNESS * LOG2_E)), 1.0)
            nw[c, j] = w
            mine = fresh[EDGE : EDGE + CHUNK]
            if j % 2:
                home[0, j // 2, pl.ds(pl.multiple_of(CHUNK * c, CHUNK), CHUNK)] = both_layers(saved, mine)
            saved = mine
        return 0

    def own_backward(c, _):
        span = pl.ds(pl.multiple_of(CHUNK * c, CHUNK), reach)
        mask = chunk_mask(c)
        q = jnp.where(mask & present(1), border[1, span], 0.0)
        saved = None
        for j in range(OWN - 1, -1, -1):
            adjoint = own_field(COTANGENT, j, span) + nw[c, j] * five(q)
            q = jnp.where(mask, adjoint * na1[c, j], 0.0)
            mine = adjoint[EDGE : EDGE + CHUNK] * na2[c, j]
            if j % 2 == 0:
                home[1, j // 2, pl.ds(pl.multiple_of(CHUNK * c, CHUNK), CHUNK)] = both_layers(mine, saved)
            saved = mine
        return 0

    def put(which):
        out = (pr_ref, gr_ref)[which]
        for n in range(OWN // 2):
            both = home[which, n].T
            out[2 * n] = both[0:ROWS]
            out[2 * n + 1] = both[ROWS:]

    swap(DESIGN, True)
    transpose_in(COTANGENT)
    for which in (DESIGN, COTANGENT):
        sides(which, True)
    for which in (DESIGN, COTANGENT):
        sides_land(which)
    rows(True)
    swap_land(DESIGN, 0)
    bands(DESIGN, 0, True)
    columns(DESIGN, 0, True)
    if last > 0:
        swap_land(DESIGN, 1)
        if direct(DESIGN, 1):
            bands(DESIGN, 1, True)
        columns(DESIGN, 1, True)
    swap(COTANGENT, True)
    for seg in range(segments):
        if seg == 0:
            w = jnp.where(inside_ref[...] > 0.5, math.exp(SHARPNESS), 1.0)
        else:
            w = taken(seg - 1, 1.0)
        weights[DEPTH * seg] = w
        if direct(DESIGN, seg):
            columns_land(DESIGN, seg)
        bands_land(DESIGN, seg)
        w = forward_segment(seg, w)
        if seg < last:
            give(seg, w)
        if seg == last:
            bands(WEIGHT, seg, True)
        columns(WEIGHT, seg, True)
        if seg < last:
            if not direct(DESIGN, seg + 1):
                columns_land(DESIGN, seg + 1)
                bands(DESIGN, seg + 1, True)
        if seg + 1 < last:
            swap_land(DESIGN, seg + 2)
            if direct(DESIGN, seg + 2):
                bands(DESIGN, seg + 2, True)
            columns(DESIGN, seg + 2, True)
        if seg > 0:
            columns_land(WEIGHT, seg - 1)
            bands(WEIGHT, seg - 1, True)
        if seg > 1:
            fill(seg - 2)
            support(seg - 2)
        if seg == max(0, last - 2):
            swap_land(COTANGENT, last)
            columns(COTANGENT, last, True)
        if seg == max(0, last - 1):
            columns_land(COTANGENT, last)
            bands(COTANGENT, last, True)
            if last > 0:
                swap_land(COTANGENT, last - 1)
                columns(COTANGENT, last - 1, True)

    if last > 0:
        columns_land(COTANGENT, last - 1)
        bands(COTANGENT, last - 1, True)
    if last > 1:
        swap_land(COTANGENT, last - 2)
        columns(COTANGENT, last - 2, True)
    if last > 0:
        fill(last - 1)
        prepare(last - 1)
    columns_land(WEIGHT, last)
    fill(last)
    prepare(last)
    for seg in range(last, -1, -1):
        if seg == last:
            q = jnp.zeros((REGION, LANES), jnp.float32)
        else:
            q = taken(last + last - 1 - seg, 0.0)
            pullbacks[per_segment * (seg + 1) - 1] = own_of(q, 0)
        bands_land(COTANGENT, seg)
        q = backward_segment(seg, q)
        if seg > 0:
            give(last + last - seg, q)
        lift(seg)
        if seg > 1:
            columns_land(COTANGENT, seg - 2)
            bands(COTANGENT, seg - 2, True)
        if seg > 2:
            swap_land(COTANGENT, seg - 3)
            columns(COTANGENT, seg - 3, True)
        if seg > 1:
            prepare(seg - 2)
        if seg == max(0, last - 1):
            for other in range(max(0, last - 1), last + 1):
                support(other)
    rows_land()
    border_land(0)
    lax.fori_loop(0, width // CHUNK, own_forward, 0)
    put(0)

    for which in (DESIGN, COTANGENT):
        swap(which, False)
        sides(which, False)
    for seg in range(segments):
        for which in (DESIGN, COTANGENT, WEIGHT):
            columns(which, seg, False)
            bands(which, seg, False)
    for n in range(2 * last):
        sync(n, False)
    rows(False)
    for p in range(1, planes):
        piece(0, p, False)
    for p in range(per_segment, planes - 1):
        piece(1, p, False)

    border_land(1)
    lax.fori_loop(0, width // CHUNK, own_backward, 0)
    put(1)
    for p in range(min(per_segment, planes - 1)):
        piece(1, p, False)


def local(design, cotangent):
    shard = jax.ShapeDtypeStruct(design.shape, jnp.float32)
    planes = lax.axis_size("build")
    layers = planes * OWN
    segments = layers // DEPTH
    width = planes * STRIP
    chunks = width // CHUNK
    syncs = max(1, 2 * (segments - 1))
    f32 = lambda *shape: pltpu.VMEM(shape, jnp.float32)
    dma = lambda *shape: pltpu.SemaphoreType.DMA(shape)
    anywhere = pl.BlockSpec(memory_space=pl.ANY)
    vmem = pl.BlockSpec(memory_space=pltpu.VMEM)
    return pl.pallas_call(
        kernel,
        out_shape=(shard, shard),
        in_specs=[anywhere, anywhere],
        out_specs=(vmem, vmem),
        scratch_shapes=[
            f32(2, OWN, ROWS, width),
            f32(2, OWN // 2, width + 2 * EDGE, LANES),
            f32(3, layers // 2, REGION, LANES),
            f32(3, 2, layers // 8, REGION, LANES),
            f32(3, 2, layers // 8, REGION, LANES),
            f32(layers + 1, REGION, LANES),
            f32(layers, REGION, LANES),
            f32(syncs, STRIP, LANES),
            f32(syncs, 3, REGION, LANES),
            f32(REGION, LANES),
            f32(2, width + 2 * EDGE, LANES),
            f32(2, width + 2 * EDGE, LANES),
            f32(2, width + 2 * EDGE, LANES),
            f32(planes, STRIP, LANES),
            f32(chunks, OWN, CHUNK + 2 * EDGE, LANES),
            f32(chunks, OWN, CHUNK + 2 * EDGE, LANES),
            f32(chunks, OWN, CHUNK, LANES),
            f32(2, OWN // 2, width, LANES),
            dma(2),
            dma(2, planes),
            dma(2, planes),
            dma(3, segments, 2, 2),
            dma(3, segments, 2, 2),
            dma(3, segments, 2, 3),
            dma(3, segments, 2, 3),
            dma(syncs, 3, 3),
            dma(syncs, 3, 3),
            dma(2, 2),
            dma(2, 2),
            dma(2),
            dma(2),
            dma(2, planes),
            dma(2, planes),
            dma(2, planes),
            dma(2, 2),
        ],
        compiler_params=pltpu.CompilerParams(
            collective_id=0, has_side_effects=True, vmem_limit_bytes=40 * 1024 * 1024
        ),
    )(design, cotangent)


def solution(mesh):
    spec = P("build", "gx", "gy")
    return jax.shard_map(local, mesh=mesh, in_specs=(spec, spec), out_specs=(spec, spec), check_vma=False)
```
